32 devices in a mesh: row: 8 (over z, y), vec: 4 (over x, core).
Axes of the slice: x: 2, y: 2, z: 4, core: 2. Of those that a mesh axis runs over, the one named last changes fastest.
Arguments:
- vectors: float32 [8192, 6144], P('row', 'vec'), may hold values from -6 to 6
- reflectors: float32 [32, 512, 256], P('row', 'vec'), may hold values from -0.25 to 0.25
- inner_factors: float32 [32, 256, 256], P('row', 'vec'), may hold values from -0.375 to 0.375
- offsets: int32 [2, 16], P(None, 'row'), may hold values from 0 to 7680, as said below
- owners: int32 [2, 16], P(None, 'row'), may hold values from 0 to 3, as said below
Outputs:
- result: float32 [8192, 6144], P('row', 'vec')
The draws below stay inside these ranges and needn't reach their ends.
Inputs may be any that keep to these rules, and one draw needn't show every extreme that they name: `offsets`: within each sweep the columns j * 2 to (j + 1) * 2 - 1 belong to panel j, the rows j * 1024 to (j + 1) * 1024 - 1; a panel's start rows increase and are multiples of 256. A first-sweep block lies within its panel. A second-sweep block starts 256 rows or more after its panel's first row; in every panel but the last, the last second-sweep block starts at the panel's end minus 256, so it runs 256 rows into the next panel; the last panel's second-sweep blocks lie within it. `owners`: for each panel, its 4 entries (both sweeps) are a permutation of 0 to 3.
All inputs are finite; a program needn't handle non-finite values.
Results may differ from the reference program's by a relative error of at most 0.0001.
Values sent between devices are 32-bit elements; how exact they have to be, the bound alone decides.
A program may use at most 64 MiB of HBM per device.

```python
import jax
import jax.numpy as jnp
from jax import lax

M = 6144
BROWS = 512
NREF = 256
BPS = 2
ROWS_DEV = 1024
N = 8192
NBLK = 16
STORED = 32


def choose(key, pool, take):
    order = jax.random.permutation(key, pool).astype(jnp.int32)
    return jnp.sort(order[:take])


def draw_offsets(key, part):
    key = jax.random.fold_in(key, 7)
    steps_dev = ROWS_DEV // NREF
    panels = NBLK // BPS

    def one_panel(panel_index):
        first_key = jax.random.fold_in(key, 2 * panel_index)
        second_key = jax.random.fold_in(key, 2 * panel_index + 1)
        middle = choose(first_key, steps_dev - 3, BPS - 2) + 1
        first_sweep = jnp.concatenate([jnp.zeros((1,), jnp.int32), middle, jnp.full((1,), steps_dev - 2, jnp.int32)])
        regular_steps = jnp.concatenate([choose(second_key, steps_dev - 2, BPS - 1) + 1, jnp.full((1,), steps_dev - 1, jnp.int32)])
        final_steps = jnp.concatenate([choose(second_key, steps_dev - 3, BPS - 1) + 1, jnp.full((1,), steps_dev - 2, jnp.int32)])
        second_sweep = jnp.where(panel_index == panels - 1, final_steps, regular_steps)
        both = jnp.stack([first_sweep, second_sweep]) * NREF + panel_index * ROWS_DEV
        return both.astype(jnp.int32)
    stacked = jax.vmap(one_panel)(jnp.arange(panels, dtype=jnp.int32))
    return jnp.transpose(stacked, (1, 0, 2)).reshape(2, NBLK)


def draw_owners(key, part):
    key = jax.random.fold_in(key, 11)
    panels = NBLK // BPS

    def one_panel(panel_index):
        order = jax.random.permutation(jax.random.fold_in(key, panel_index), 2 * BPS)
        return order.astype(jnp.int32).reshape(2, BPS)
    stacked = jax.vmap(one_panel)(jnp.arange(panels, dtype=jnp.int32))
    return jnp.transpose(stacked, (1, 0, 2)).reshape(2, NBLK)


def level_of(own_key, shape, split, least, high):
    factor_of = 1.0
    for axis_at, blocks in split:
        draws = jax.random.uniform(jax.random.fold_in(jax.random.fold_in(own_key, 6), axis_at), (blocks,), jnp.float32, least / len(split), high / len(split))
        factor_of = factor_of * jnp.repeat(jnp.exp(draws), shape[axis_at] // blocks).reshape((-1,) + (1,) * (len(shape) - 1 - axis_at))
    return factor_of


def normal_values(rng, shape, scale, bound, shards=(), held_as=jnp.bfloat16):
    factor_of = level_of(rng, shape, shards, -0.22, 0.18) if shards else 1.0
    result = jax.random.normal(rng, shape, jnp.float32) * scale * factor_of
    return jnp.minimum(jnp.maximum(result, -bound), bound).astype(held_as)


def setup_inputs(seed: int = 0) -> dict:
    arg_keys = jax.random.split(jax.random.key(seed), 6)
    vectors = normal_values(arg_keys[0], (N, M), 1.0, 6.0, ((0, 8), (1, 4)), jnp.float32)
    reflectors = normal_values(arg_keys[1], (STORED, BROWS, NREF), BROWS ** -0.5, 0.25, ((0, 8), (1, 4)), jnp.float32)
    inner_factors = normal_values(arg_keys[2], (STORED, NREF, NREF), NREF ** -0.5, 0.375, ((0, 8), (1, 4)), jnp.float32)
    offsets = draw_offsets(jax.random.fold_in(arg_keys[5], 71), 0)
    owners = draw_owners(jax.random.fold_in(arg_keys[5], 71), 0)
    return dict(vectors=vectors, reflectors=reflectors, inner_factors=inner_factors, offsets=offsets, owners=owners)


def contract_rows(left, right):
    return lax.dot_general(left, right, (((0,), (0,)), ((), ())), precision=lax.Precision.HIGHEST, preferred_element_type=jnp.float32)


def multiply(left, right):
    return jnp.dot(left, right, precision=lax.Precision.HIGHEST, preferred_element_type=jnp.float32)


def reference(vectors, reflectors, inner_factors, offsets, owners):
    def make_sweep(sweep_index):
        def apply_block(block_index, current):
            block_index = jnp.asarray(block_index).astype(jnp.int32)
            start_row = offsets[sweep_index, block_index].astype(jnp.int32)
            stored_at = ((block_index // BPS) * (2 * BPS) + owners[sweep_index, block_index]).astype(jnp.int32)
            basis_block = lax.dynamic_index_in_dim(reflectors, stored_at, 0, keepdims=False)
            inner_block = lax.dynamic_index_in_dim(inner_factors, stored_at, 0, keepdims=False)
            window = lax.dynamic_slice_in_dim(current, start_row, BROWS, 0)
            projection = contract_rows(basis_block, window)
            coupled = multiply(inner_block, projection)
            window = window - multiply(basis_block, coupled)
            return lax.dynamic_update_slice_in_dim(current, window, start_row, 0)
        return apply_block

    current = vectors
    for sweep_index in range(2):
        current = lax.fori_loop(0, NBLK, make_sweep(sweep_index), current)
    return current
```

```python
import functools

import jax
import jax.numpy as jnp
from jax import lax
from jax.experimental import pallas as pl
from jax.experimental.pallas import tpu as pltpu
from jax.sharding import PartitionSpec as P

MESH = pl.DeviceIdType.MESH


def split(value):
    high = value.astype(jnp.bfloat16)
    low = (value - high.astype(jnp.float32)).astype(jnp.bfloat16)
    return high, low


def dot(left, right):
    return jnp.dot(left, right, preferred_element_type=jnp.float32)


def dot_split(left_high, left_low, right):
    right_high, right_low = split(right)
    return dot(left_high, right_high) + (dot(left_high, right_low) + dot(left_low, right_high))


def kernel(
    panels, members, per_sweep, step, chunks, width,
    places, owners, vectors, reflectors, inner, out,
    current, below, update, gathered, basis_high, basis_low, mixed_high, mixed_low,
    load_sem, store_sem, head_sem, part_send, part_recv, back_send, back_recv, fore_send, fore_recv,
):
    panel = lax.axis_index("row")
    me = lax.axis_index("vec")
    core = lax.rem(me, 2)
    chip = me // 2
    chips = members // 2
    sibling = chip * 2 + 1 - core
    units = vectors.shape[0]
    basis_rows = reflectors.shape[1]
    is_first = panel == 0
    is_last = panel == panels - 1
    stored = [(sweep, index) for sweep in range(2) for index in range(per_sweep)]

    def columns(chunk):
        return pl.ds(pl.multiple_of(chunk * width, width), width)

    def load(chunk):
        return pltpu.make_async_copy(vectors.at[:, :, columns(chunk)], current.at[chunk], load_sem.at[chunk])

    def store(chunk):
        return pltpu.make_async_copy(
            current.at[chunk, pl.ds(1, units - 1)],
            out.at[pl.ds(1, units - 1), :, columns(chunk)],
            store_sem.at[chunk],
        )

    def store_head(chunk):
        return pltpu.make_async_copy(
            current.at[chunk, 0], out.at[0, :, columns(chunk)], head_sem.at[chunk]
        )

    def send_back(chunk):
        return pltpu.make_async_remote_copy(
            src_ref=current.at[chunk, 0],
            dst_ref=below.at[chunk],
            send_sem=back_send.at[chunk],
            recv_sem=back_recv.at[chunk],
            device_id=(panel - 1, me),
            device_id_type=MESH,
        )

    def send_fore(chunk):
        return pltpu.make_async_remote_copy(
            src_ref=below.at[chunk],
            dst_ref=out.at[0, :, columns(chunk)],
            send_sem=fore_send.at[chunk],
            recv_sem=fore_recv.at[chunk],
            device_id=(panel + 1, me),
            device_id_type=MESH,
        )

    def send_part(block, part, slot, target):
        return pltpu.make_async_remote_copy(
            src_ref=gathered.at[block, part],
            dst_ref=gathered.at[block, part],
            send_sem=part_send.at[block, slot],
            recv_sem=part_recv.at[block, part],
            device_id=(panel, target),
            device_id_type=MESH,
        )

    def other_chip(distance):
        return lax.rem(chip + distance, chips)

    def each(body):
        lax.fori_loop(0, chunks, lambda chunk, _: (body(chunk), 0)[1], 0)

    each(lambda chunk: load(chunk).start())

    barrier = pltpu.get_barrier_semaphore()

    def greet(row, vec):
        pl.semaphore_signal(barrier, inc=1, device_id=(row, vec), device_id_type=MESH)

    greet(panel, sibling)
    for distance in range(1, chips):
        greet(panel, other_chip(distance) * 2 + core)

    @pl.when(jnp.logical_not(is_first))
    def _():
        greet(panel - 1, me)

    @pl.when(jnp.logical_not(is_last))
    def _():
        greet(panel + 1, me)

    for block, (sweep, index) in enumerate(stored):
        owner = owners[sweep, index]
        gathered[block, me, :basis_rows, :] = reflectors[owner]
        gathered[block, me, basis_rows:, :] = inner[owner]

    update[0] = jnp.zeros_like(update[0])
    update[3] = jnp.zeros_like(update[3])

    pl.semaphore_wait(barrier, chips + jnp.minimum(panel, 1) + jnp.minimum(panels - 1 - panel, 1))

    for block in range(len(stored)):
        for distance in range(1, chips):
            send_part(block, me, distance, other_chip(distance) * 2 + core).start()
        send_part(block, me, 0, sibling).start()

    def fetch(block):
        for distance in range(1, chips):
            part = other_chip(distance) * 2 + core
            send_part(block, part, distance, part).wait_recv()
            send_part(block, part, chips - 1 + distance, sibling).start()
        send_part(block, sibling, 0, sibling).wait_recv()
        for distance in range(1, chips):
            part = other_chip(distance) * 2 + 1 - core
            send_part(block, part, chips - 1 + distance, sibling).wait_recv()
        basis = gathered[block, :, :basis_rows, :].reshape(2 * step, step)
        coupling = gathered[block, :, basis_rows:, :].reshape(step, step)
        high, low = split(basis)
        mixed_high[block], mixed_low[block] = split(dot_split(high, low, coupling))
        basis_high[block], basis_low[block] = split(basis.T)

    def change(block, upper, lower):
        window = jnp.concatenate([upper, lower], 0)
        projection = dot_split(basis_high[block], basis_low[block], window)
        moved = dot_split(mixed_high[block], mixed_low[block], projection)
        update[1] = moved[:step]
        update[2] = moved[step:]

    def apply_change(block, chunk, lowest):
        for unit in range(lowest, units):
            current[chunk, unit] = current[chunk, unit] - update[places[block, 2 + unit]]

    each(lambda chunk: load(chunk).wait())

    for block, (sweep, index) in enumerate(stored[:-1]):
        fetch(block)

        def run(chunk, block=block, lowest=sweep + index):
            change(block, current[chunk, places[block, 0]], current[chunk, places[block, 1]])
            apply_change(block, chunk, lowest)
            if block == 0:

                @pl.when(jnp.logical_not(is_first))
                def _():
                    send_back(chunk).start()

                @pl.when(is_first)
                def _():
                    store_head(chunk).start()

        each(run)

    last = len(stored) - 1
    fetch(last)

    def finish(chunk):
        @pl.when(is_last)
        def _():
            below[chunk] = current[chunk, places[last, 1]]

        @pl.when(jnp.logical_not(is_last))
        def _():
            send_back(chunk).wait_recv()

        change(last, current[chunk, places[last, 0]], below[chunk])

        @pl.when(jnp.logical_not(is_last))
        def _():
            below[chunk] = below[chunk] - update[2]
            send_fore(chunk).start()

        apply_change(last, chunk, per_sweep)
        store(chunk).start()

    each(finish)

    for block in range(len(stored)):
        for slot in range(members - 1):
            send_part(block, me, slot, sibling).wait_send()

    @pl.when(is_first)
    def _():
        each(lambda chunk: store_head(chunk).wait())

    @pl.when(jnp.logical_not(is_first))
    def _():
        each(lambda chunk: send_back(chunk).wait_send())

    each(lambda chunk: store(chunk).wait())

    @pl.when(jnp.logical_not(is_last))
    def _():
        each(lambda chunk: send_fore(chunk).wait_send())

    @pl.when(jnp.logical_not(is_first))
    def _():
        each(lambda chunk: send_fore(chunk).wait_recv())


def shards(panels, members, vectors, reflectors, inner_factors, offsets, owners):
    rows_dev, cols = vectors.shape
    blocks, basis_rows, step = reflectors.shape
    inner_rows = inner_factors.shape[1]
    per_sweep = offsets.shape[1]
    width = 256 if cols % 256 == 0 else 128
    chunks = cols // width
    units = rows_dev // step
    first_unit = (offsets - lax.axis_index("row") * rows_dev).reshape(-1, 1) // step
    unit_at = jnp.arange(units, dtype=jnp.int32)
    places = jnp.concatenate(
        [first_unit, jnp.minimum(first_unit + 1, units - 1), jnp.clip(unit_at - first_unit + 1, 0, 3)], 1
    )
    smem = pl.BlockSpec(memory_space=pltpu.SMEM)
    vmem = pl.BlockSpec(memory_space=pltpu.VMEM)
    anywhere = pl.BlockSpec(memory_space=pl.ANY)
    dma = pltpu.SemaphoreType.DMA
    result = pl.pallas_call(
        functools.partial(kernel, panels, members, per_sweep, step, chunks, width),
        out_shape=jax.ShapeDtypeStruct((units, step, cols), jnp.float32),
        in_specs=[smem, smem, anywhere, vmem, vmem],
        out_specs=anywhere,
        scratch_shapes=[
            pltpu.VMEM((chunks, units, step, width), jnp.float32),
            pltpu.VMEM((chunks, step, width), jnp.float32),
            pltpu.VMEM((4, step, width), jnp.float32),
            pltpu.VMEM((blocks, members, basis_rows + inner_rows, step), jnp.float32),
            pltpu.VMEM((blocks, step, 2 * step), jnp.bfloat16),
            pltpu.VMEM((blocks, step, 2 * step), jnp.bfloat16),
            pltpu.VMEM((blocks, 2 * step, step), jnp.bfloat16),
            pltpu.VMEM((blocks, 2 * step, step), jnp.bfloat16),
            dma((chunks,)),
            dma((chunks,)),
            dma((chunks,)),
            dma((blocks, members - 1)),
            dma((blocks, members)),
            dma((chunks,)),
            dma((chunks,)),
            dma((chunks,)),
            dma((chunks,)),
        ],
        compiler_params=pltpu.CompilerParams(
            collective_id=0, has_side_effects=True, vmem_limit_bytes=48 * 1024 * 1024
        ),
        cost_estimate=pl.CostEstimate(
            flops=2 * 3 * 4 * blocks * step * step * cols,
            bytes_accessed=2 * 4 * rows_dev * cols,
            transcendentals=0,
        ),
    )(places, owners, vectors.reshape(units, step, cols), reflectors, inner_factors)
    return result.reshape(rows_dev, cols)


def solution(mesh):
    return jax.shard_map(
        functools.partial(shards, mesh.shape["row"], mesh.shape["vec"]),
        mesh=mesh,
        in_specs=(
            P("row", "vec"),
            P("row", "vec", None),
            P("row", "vec", None),
            P(None, "row"),
            P(None, "row"),
        ),
        out_specs=P("row", "vec"),
        check_vma=False,
    )
```

```python
import functools

import jax
import jax.numpy as jnp
from jax import lax
from jax.experimental import pallas as pl
from jax.experimental.pallas import tpu as pltpu
from jax.sharding import PartitionSpec as P

MESH = pl.DeviceIdType.MESH


def split(value):
    high = value.astype(jnp.bfloat16)
    low = (value - high.astype(jnp.float32)).astype(jnp.bfloat16)
    return high, low


def dot(left, right):
    return jnp.dot(left, right, preferred_element_type=jnp.float32)


def dot_split(left_high, left_low, right):
    right_high, right_low = split(right)
    return dot(left_high, right_high) + (dot(left_high, right_low) + dot(left_low, right_high))


def kernel(
    panels, members, per_sweep, step, chunks, width,
    offsets_in, owners_in, vectors, reflectors_in, inner_in, out,
    offsets, owners, reflectors, inner, relay, current, below, update, gathered, basis_high, basis_low, mixed_high, mixed_low,
    early_sem, relay_send, relay_recv, load_sem, store_sem, head_sem, part_send, part_recv, back_send, back_recv, fore_send, fore_recv,
):
    panel = lax.axis_index("row")
    me = lax.axis_index("vec")
    core = lax.rem(me, 2)
    chip = me // 2
    chips = members // 2
    sibling = chip * 2 + 1 - core
    units = vectors.shape[0]
    basis_rows = reflectors.shape[1]
    first_row = panel * units * step
    pairs = panels // 2
    is_odd = panel % 2 == 1
    pair = panel // 2
    is_first = panel == 0
    is_last = panel == panels - 1
    stored = [(sweep, index) for sweep in range(2) for index in range(per_sweep)]

    def columns(chunk):
        return pl.ds(pl.multiple_of(chunk * width, width), width)

    def load(chunk):
        return pltpu.make_async_copy(vectors.at[:, :, columns(chunk)], current.at[chunk], load_sem.at[chunk])

    def store(chunk):
        return pltpu.make_async_copy(
            current.at[chunk, pl.ds(1, units - 1)],
            out.at[pl.ds(1, units - 1), :, columns(chunk)],
            store_sem.at[chunk],
        )

    def store_head(chunk):
        return pltpu.make_async_copy(
            current.at[chunk, 0], out.at[0, :, columns(chunk)], head_sem.at[chunk]
        )

    def turn(chunk, share):
        return ((chunk + 1) * share) // pairs - (chunk * share) // pairs == 1

    def back_turn(chunk, source_pair):
        return turn(chunk, pairs - source_pair)

    def fore_turn(chunk, source_pair):
        return turn(chunk, source_pair + 1)

    def remote(source, target, send_sem, recv_sem, row):
        return pltpu.make_async_remote_copy(
            src_ref=source,
            dst_ref=target,
            send_sem=send_sem,
            recv_sem=recv_sem,
            device_id=(row, me),
            device_id_type=MESH,
        )

    def head(chunk):
        return out.at[0, :, columns(chunk)]

    def send_back(chunk):
        return remote(current.at[chunk, 0], below.at[chunk], back_send.at[chunk], back_recv.at[chunk], panel - 1)

    def send_back_far(chunk):
        return remote(current.at[chunk, 0], relay.at[chunk], back_send.at[chunk], relay_recv.at[chunk], panel - 2)

    def send_fore(chunk):
        return remote(below.at[chunk], head(chunk), fore_send.at[chunk], fore_recv.at[chunk], panel + 1)

    def send_fore_far(chunk):
        return remote(below.at[chunk], relay.at[chunk], fore_send.at[chunk], relay_recv.at[chunk], panel + 2)

    def pass_back(chunk):
        return remote(relay.at[chunk], below.at[chunk], relay_send.at[chunk], back_recv.at[chunk], panel + 1)

    def pass_fore(chunk):
        return remote(relay.at[chunk], head(chunk), relay_send.at[chunk], fore_recv.at[chunk], panel - 1)

    passes_back = jnp.logical_and(jnp.logical_not(is_odd), panel + 2 < panels)
    passes_fore = jnp.logical_and(is_odd, panel > 1)

    def both(left, right):
        return jnp.logical_and(left, right)

    def start_back(chunk):
        far = both(jnp.logical_not(is_odd), back_turn(chunk, pair))

        @pl.when(far)
        def _():
            send_back_far(chunk).start()

        @pl.when(jnp.logical_not(far))
        def _():
            send_back(chunk).start()

    def start_fore(chunk):
        far = both(both(is_odd, panel + 2 < panels), fore_turn(chunk, pair))

        @pl.when(far)
        def _():
            send_fore_far(chunk).start()

        @pl.when(jnp.logical_not(far))
        def _():
            send_fore(chunk).start()

    def hand_back(chunk):
        @pl.when(both(passes_back, both(chunk < chunks, back_turn(chunk, pair + 1))))
        def _():
            send_back_far(chunk).wait_recv()
            pass_back(chunk).start()

    def hand_fore(chunk):
        @pl.when(both(passes_fore, both(chunk >= 0, fore_turn(chunk, pair - 1))))
        def _():
            send_fore_far(chunk).wait_recv()
            pass_fore(chunk).start()

    def settle(chunk):
        handed = jnp.logical_or(
            both(passes_back, back_turn(chunk, pair + 1)), both(passes_fore, fore_turn(chunk, pair - 1))
        )

        @pl.when(handed)
        def _():
            pass_back(chunk).wait_send()

    def send_part(block, part, slot, target):
        return pltpu.make_async_remote_copy(
            src_ref=gathered.at[block, part],
            dst_ref=gathered.at[block, part],
            send_sem=part_send.at[block, slot],
            recv_sem=part_recv.at[block, part],
            device_id=(panel, target),
            device_id_type=MESH,
        )

    def other_chip(distance):
        return lax.rem(chip + distance, chips)

    def each(body):
        lax.fori_loop(0, chunks, lambda chunk, _: (body(chunk), 0)[1], 0)

    early = [
        pltpu.make_async_copy(source, target, early_sem.at[at])
        for at, (source, target) in enumerate(
            [(owners_in, owners), (offsets_in, offsets), (reflectors_in, reflectors), (inner_in, inner)]
        )
    ]
    for copy in early:
        copy.start()
    each(lambda chunk: load(chunk).start())

    barrier = pltpu.get_barrier_semaphore()

    def greet(row, vec):
        pl.semaphore_signal(barrier, inc=1, device_id=(row, vec), device_id_type=MESH)

    greet(panel, sibling)
    for distance in range(1, chips):
        greet(panel, other_chip(distance) * 2 + core)

    @pl.when(jnp.logical_not(is_first))
    def _():
        greet(panel - 1, me)

    @pl.when(jnp.logical_not(is_last))
    def _():
        greet(panel + 1, me)

    @pl.when(panel > 1)
    def _():
        greet(panel - 2, me)

    @pl.when(panel + 2 < panels)
    def _():
        greet(panel + 2, me)

    for copy in early:
        copy.wait()

    for block, (sweep, index) in enumerate(stored):
        owner = owners[sweep, index]
        gathered[block, me, :basis_rows, :] = reflectors[owner]
        gathered[block, me, basis_rows:, :] = inner[owner]

    update[0] = jnp.zeros_like(update[0])
    update[3] = jnp.zeros_like(update[3])

    beside = jnp.minimum(panel, 1) + jnp.minimum(panels - 1 - panel, 1)
    beyond = jnp.minimum(panel // 2, 1) + jnp.minimum((panels - 1 - panel) // 2, 1)
    pl.semaphore_wait(barrier, chips + beside + beyond)

    for block in range(len(stored)):
        for distance in range(1, chips):
            send_part(block, me, distance, other_chip(distance) * 2 + core).start()
        send_part(block, me, 0, sibling).start()

    def fetch(block):
        for distance in range(1, chips):
            part = other_chip(distance) * 2 + core
            send_part(block, part, distance, part).wait_recv()
            send_part(block, part, chips - 1 + distance, sibling).start()
        send_part(block, sibling, 0, sibling).wait_recv()
        for distance in range(1, chips):
            part = other_chip(distance) * 2 + 1 - core
            send_part(block, part, chips - 1 + distance, sibling).wait_recv()
        basis = gathered[block, :, :basis_rows, :].reshape(2 * step, step)
        coupling = gathered[block, :, basis_rows:, :].reshape(step, step)
        high, low = split(basis)
        mixed_high[block], mixed_low[block] = split(dot_split(high, low, coupling))
        basis_high[block], basis_low[block] = split(basis.T)

    def change(block, upper, lower):
        window = jnp.concatenate([upper, lower], 0)
        projection = dot_split(basis_high[block], basis_low[block], window)
        moved = dot_split(mixed_high[block], mixed_low[block], projection)
        update[1] = moved[:step]
        update[2] = moved[step:]

    def first_unit(block):
        return jnp.maximum(offsets[stored[block][0], stored[block][1]] - first_row, 0) // step

    def lower_unit(block):
        return jnp.minimum(first_unit(block) + 1, units - 1)

    def apply_change(block, chunk, lowest):
        first = first_unit(block)
        for unit in range(lowest, units):
            place = jnp.minimum(jnp.maximum(unit + 1 - first, 0), 3)
            current[chunk, unit] = current[chunk, unit] - update[place]

    each(lambda chunk: load(chunk).wait())

    for block, (sweep, index) in enumerate(stored[:-1]):
        fetch(block)

        def run(chunk, block=block, lowest=sweep + index):
            change(block, current[chunk, first_unit(block)], current[chunk, lower_unit(block)])
            apply_change(block, chunk, lowest)
            if block == 0:

                @pl.when(jnp.logical_not(is_first))
                def _():
                    start_back(chunk)

                @pl.when(is_first)
                def _():
                    store_head(chunk).start()

        each(run)

    last = len(stored) - 1
    fetch(last)

    def finish(chunk):
        @pl.when(is_last)
        def _():
            below[chunk] = current[chunk, lower_unit(last)]

        @pl.when(jnp.logical_not(is_last))
        def _():
            send_back(chunk).wait_recv()

        change(last, current[chunk, first_unit(last)], below[chunk])

        @pl.when(jnp.logical_not(is_last))
        def _():
            below[chunk] = below[chunk] - update[2]
            start_fore(chunk)

        hand_back(chunk + 1)
        hand_fore(chunk - 1)
        apply_change(last, chunk, per_sweep)
        store(chunk).start()

    hand_back(0)
    each(finish)
    hand_fore(chunks - 1)
    each(settle)

    for block in range(len(stored)):
        for slot in range(members - 1):
            send_part(block, me, slot, sibling).wait_send()

    @pl.when(is_first)
    def _():
        each(lambda chunk: store_head(chunk).wait())

    @pl.when(jnp.logical_not(is_first))
    def _():
        each(lambda chunk: send_back(chunk).wait_send())

    each(lambda chunk: store(chunk).wait())

    @pl.when(jnp.logical_not(is_last))
    def _():
        each(lambda chunk: send_fore(chunk).wait_send())

    @pl.when(jnp.logical_not(is_first))
    def _():
        each(lambda chunk: send_fore(chunk).wait_recv())


def shards(panels, members, vectors, reflectors, inner_factors, offsets, owners):
    rows_dev, cols = vectors.shape
    blocks, basis_rows, step = reflectors.shape
    inner_rows = inner_factors.shape[1]
    per_sweep = offsets.shape[1]
    width = 128
    chunks = cols // width
    units = rows_dev // step
    anywhere = pl.BlockSpec(memory_space=pl.ANY)
    dma = pltpu.SemaphoreType.DMA
    result = pl.pallas_call(
        functools.partial(kernel, panels, members, per_sweep, step, chunks, width),
        out_shape=jax.ShapeDtypeStruct((units, step, cols), jnp.float32),
        in_specs=[anywhere] * 5,
        out_specs=anywhere,
        scratch_shapes=[
            pltpu.SMEM(offsets.shape, jnp.int32),
            pltpu.SMEM(owners.shape, jnp.int32),
            pltpu.VMEM(reflectors.shape, jnp.float32),
            pltpu.VMEM(inner_factors.shape, jnp.float32),
            pltpu.VMEM((chunks, step, width), jnp.float32),
            pltpu.VMEM((chunks, units, step, width), jnp.float32),
            pltpu.VMEM((chunks, step, width), jnp.float32),
            pltpu.VMEM((4, step, width), jnp.float32),
            pltpu.VMEM((blocks, members, basis_rows + inner_rows, step), jnp.float32),
            pltpu.VMEM((blocks, step, 2 * step), jnp.bfloat16),
            pltpu.VMEM((blocks, step, 2 * step), jnp.bfloat16),
            pltpu.VMEM((blocks, 2 * step, step), jnp.bfloat16),
            pltpu.VMEM((blocks, 2 * step, step), jnp.bfloat16),
            dma((4,)),
            dma((chunks,)),
            dma((chunks,)),
            dma((chunks,)),
            dma((chunks,)),
            dma((chunks,)),
            dma((blocks, members - 1)),
            dma((blocks, members)),
            dma((chunks,)),
            dma((chunks,)),
            dma((chunks,)),
            dma((chunks,)),
        ],
        compiler_params=pltpu.CompilerParams(
            collective_id=0, has_side_effects=True, vmem_limit_bytes=48 * 1024 * 1024
        ),
        cost_estimate=pl.CostEstimate(
            flops=2 * 3 * 4 * blocks * step * step * cols,
            bytes_accessed=2 * 4 * rows_dev * cols,
            transcendentals=0,
        ),
    )(offsets, owners, vectors.reshape(units, step, cols), reflectors, inner_factors)
    return result.reshape(rows_dev, cols)


def solution(mesh):
    return jax.shard_map(
        functools.partial(shards, mesh.shape["row"], mesh.shape["vec"]),
        mesh=mesh,
        in_specs=(
            P("row", "vec"),
            P("row", "vec", None),
            P("row", "vec", None),
            P(None, "row"),
            P(None, "row"),
        ),
        out_specs=P("row", "vec"),
        check_vma=False,
    )
```

```python
import functools

import jax
import jax.numpy as jnp
from jax import lax
from jax.experimental import pallas as pl
from jax.experimental.pallas import tpu as pltpu
from jax.sharding import PartitionSpec as P

MESH = pl.DeviceIdType.MESH


def split(value):
    high = value.astype(jnp.bfloat16)
    low = (value - high.astype(jnp.float32)).astype(jnp.bfloat16)
    return high, low


def dot(left, right):
    return jnp.dot(left, right, preferred_element_type=jnp.float32)


def dot_split(left_high, left_low, right):
    right_high, right_low = split(right)
    return dot(left_high, right_high) + (dot(left_high, right_low) + dot(left_low, right_high))


def kernel(
    panels, members, per_sweep, step, chunks, width,
    offsets_in, owners_in, vectors, reflectors_in, inner_in, out,
    offsets, owners, reflectors, inner, relay, current, below, update, gathered, basis_high, basis_low, mixed_high, mixed_low,
    early_sem, relay_send, relay_recv, load_sem, store_sem, head_sem, part_send, part_recv, back_send, back_recv, fore_send, fore_recv,
):
    panel = lax.axis_index("row")
    me = lax.axis_index("vec")
    core = lax.rem(me, 2)
    chip = me // 2
    chips = members // 2
    sibling = chip * 2 + 1 - core
    units = vectors.shape[0]
    basis_rows = reflectors.shape[1]
    first_row = panel * units * step
    pairs = panels // 2
    is_odd = panel % 2 == 1
    pair = panel // 2
    is_first = panel == 0
    is_last = panel == panels - 1
    stored = [(sweep, index) for sweep in range(2) for index in range(per_sweep)]

    def columns(chunk):
        return pl.ds(pl.multiple_of(chunk * width, width), width)

    def load(chunk):
        return pltpu.make_async_copy(vectors.at[:, :, columns(chunk)], current.at[chunk], load_sem.at[chunk])

    def store(chunk):
        return pltpu.make_async_copy(
            current.at[chunk, pl.ds(1, units - 1)],
            out.at[pl.ds(1, units - 1), :, columns(chunk)],
            store_sem.at[chunk],
        )

    def store_head(chunk):
        return pltpu.make_async_copy(
            current.at[chunk, 0], out.at[0, :, columns(chunk)], head_sem.at[chunk]
        )

    def turn(chunk, share):
        return ((chunk + 1) * share) // pairs - (chunk * share) // pairs == 1

    def back_turn(chunk, source_pair):
        return turn(chunk, pairs - source_pair)

    def fore_turn(chunk, source_pair):
        return turn(chunk, source_pair + 1)

    def remote(source, target, send_sem, recv_sem, row):
        return pltpu.make_async_remote_copy(
            src_ref=source,
            dst_ref=target,
            send_sem=send_sem,
            recv_sem=recv_sem,
            device_id=(row, me),
            device_id_type=MESH,
        )

    def head(chunk):
        return out.at[0, :, columns(chunk)]

    def send_back(chunk):
        return remote(current.at[chunk, 0], below.at[chunk], back_send.at[chunk], back_recv.at[chunk], panel - 1)

    def send_back_far(chunk):
        return remote(current.at[chunk, 0], relay.at[chunk], back_send.at[chunk], relay_recv.at[chunk], panel - 2)

    def send_fore(chunk):
        return remote(below.at[chunk], head(chunk), fore_send.at[chunk], fore_recv.at[chunk], panel + 1)

    def send_fore_far(chunk):
        return remote(below.at[chunk], relay.at[chunk], fore_send.at[chunk], relay_recv.at[chunk], panel + 2)

    def pass_back(chunk):
        return remote(relay.at[chunk], below.at[chunk], relay_send.at[chunk], back_recv.at[chunk], panel + 1)

    def pass_fore(chunk):
        return remote(relay.at[chunk], head(chunk), relay_send.at[chunk], fore_recv.at[chunk], panel - 1)

    passes_back = jnp.logical_and(jnp.logical_not(is_odd), panel + 2 < panels)
    passes_fore = jnp.logical_and(is_odd, panel > 1)

    def both(left, right):
        return jnp.logical_and(left, right)

    def start_back(chunk):
        far = both(jnp.logical_not(is_odd), back_turn(chunk, pair))

        @pl.when(far)
        def _():
            send_back_far(chunk).start()

        @pl.when(jnp.logical_not(far))
        def _():
            send_back(chunk).start()

    def start_fore(chunk):
        far = both(both(is_odd, panel + 2 < panels), fore_turn(chunk, pair))

        @pl.when(far)
        def _():
            send_fore_far(chunk).start()

        @pl.when(jnp.logical_not(far))
        def _():
            send_fore(chunk).start()

    def hand_back(chunk):
        @pl.when(both(passes_back, both(chunk < chunks, back_turn(chunk, pair + 1))))
        def _():
            send_back_far(chunk).wait_recv()
            pass_back(chunk).start()

    def hand_fore(chunk):
        @pl.when(both(passes_fore, both(chunk >= 0, fore_turn(chunk, pair - 1))))
        def _():
            send_fore_far(chunk).wait_recv()
            pass_fore(chunk).start()

    def settle(chunk):
        handed = jnp.logical_or(
            both(passes_back, back_turn(chunk, pair + 1)), both(passes_fore, fore_turn(chunk, pair - 1))
        )

        @pl.when(handed)
        def _():
            pass_back(chunk).wait_send()

    def send_part(block, part, slot, target):
        return pltpu.make_async_remote_copy(
            src_ref=gathered.at[block, part],
            dst_ref=gathered.at[block, part],
            send_sem=part_send.at[block, slot],
            recv_sem=part_recv.at[block, part],
            device_id=(panel, target),
            device_id_type=MESH,
        )

    def other_chip(distance):
        return lax.rem(chip + distance, chips)

    def each(body):
        lax.fori_loop(0, chunks, lambda chunk, _: (body(chunk), 0)[1], 0)

    early = [
        pltpu.make_async_copy(source, target, early_sem.at[at])
        for at, (source, target) in enumerate(
            [(owners_in, owners), (offsets_in, offsets), (reflectors_in, reflectors), (inner_in, inner)]
        )
    ]
    for copy in early:
        copy.start()
    each(lambda chunk: load(chunk).start())

    barrier = pltpu.get_barrier_semaphore()

    def greet(row, vec):
        pl.semaphore_signal(barrier, inc=1, device_id=(row, vec), device_id_type=MESH)

    greet(panel, sibling)
    for distance in range(1, chips):
        greet(panel, other_chip(distance) * 2 + core)

    @pl.when(jnp.logical_not(is_first))
    def _():
        greet(panel - 1, me)

    @pl.when(jnp.logical_not(is_last))
    def _():
        greet(panel + 1, me)

    @pl.when(panel > 1)
    def _():
        greet(panel - 2, me)

    @pl.when(panel + 2 < panels)
    def _():
        greet(panel + 2, me)

    for copy in early:
        copy.wait()

    for block, (sweep, index) in enumerate(stored):
        owner = owners[sweep, index]
        gathered[block, me, :basis_rows, :] = reflectors[owner]
        gathered[block, me, basis_rows:, :] = inner[owner]

    update[0] = jnp.zeros_like(update[0])
    update[3] = jnp.zeros_like(update[3])

    beside = jnp.minimum(panel, 1) + jnp.minimum(panels - 1 - panel, 1)
    beyond = jnp.minimum(panel // 2, 1) + jnp.minimum((panels - 1 - panel) // 2, 1)
    pl.semaphore_wait(barrier, chips + beside + beyond)

    for block in range(len(stored)):
        for distance in range(1, chips):
            send_part(block, me, distance, other_chip(distance) * 2 + core).start()
        send_part(block, me, 0, sibling).start()

    def fetch(block):
        for distance in range(1, chips):
            part = other_chip(distance) * 2 + core
            send_part(block, part, distance, part).wait_recv()
            send_part(block, part, chips - 1 + distance, sibling).start()
        send_part(block, sibling, 0, sibling).wait_recv()
        for distance in range(1, chips):
            part = other_chip(distance) * 2 + 1 - core
            send_part(block, part, chips - 1 + distance, sibling).wait_recv()
        basis = gathered[block, :, :basis_rows, :].reshape(2 * step, step)
        coupling = gathered[block, :, basis_rows:, :].reshape(step, step)
        high, low = split(basis)
        mixed_high[block], mixed_low[block] = split(dot_split(high, low, coupling))
        basis_high[block], basis_low[block] = split(basis.T)

    def change(block, upper, lower):
        window = jnp.concatenate([upper, lower], 0)
        projection = dot_split(basis_high[block], basis_low[block], window)
        moved = dot_split(mixed_high[block], mixed_low[block], projection)
        update[1] = moved[:step]
        update[2] = moved[step:]

    def first_unit(block):
        return jnp.maximum(offsets[stored[block][0], stored[block][1]] - first_row, 0) // step

    def lower_unit(block):
        return jnp.minimum(first_unit(block) + 1, units - 1)

    def apply_change(block, chunk, lowest):
        first = first_unit(block)
        for unit in range(lowest, units):
            place = jnp.minimum(jnp.maximum(unit + 1 - first, 0), 3)
            current[chunk, unit] = current[chunk, unit] - update[place]

    each(lambda chunk: load(chunk).wait())

    def run(block, chunk):
        change(block, current[chunk, first_unit(block)], current[chunk, lower_unit(block)])
        apply_change(block, chunk, sum(stored[block]))

    def begin(chunk):
        run(0, chunk)

        @pl.when(jnp.logical_not(is_first))
        def _():
            start_back(chunk)

        @pl.when(is_first)
        def _():
            store_head(chunk).start()

    last = len(stored) - 1
    fetch(0)
    each(begin)
    for block in range(1, len(stored)):
        fetch(block)

    def finish(chunk):
        for block in range(1, last):
            run(block, chunk)

        @pl.when(is_last)
        def _():
            below[chunk] = current[chunk, lower_unit(last)]

        @pl.when(jnp.logical_not(is_last))
        def _():
            send_back(chunk).wait_recv()

        change(last, current[chunk, first_unit(last)], below[chunk])

        @pl.when(jnp.logical_not(is_last))
        def _():
            below[chunk] = below[chunk] - update[2]
            start_fore(chunk)

        hand_back(chunk + 1)
        hand_fore(chunk - 1)
        apply_change(last, chunk, per_sweep)
        store(chunk).start()

    hand_back(0)
    each(finish)
    hand_fore(chunks - 1)
    each(settle)

    for block in range(len(stored)):
        for slot in range(members - 1):
            send_part(block, me, slot, sibling).wait_send()

    @pl.when(is_first)
    def _():
        each(lambda chunk: store_head(chunk).wait())

    @pl.when(jnp.logical_not(is_first))
    def _():
        each(lambda chunk: send_back(chunk).wait_send())

    each(lambda chunk: store(chunk).wait())

    @pl.when(jnp.logical_not(is_last))
    def _():
        each(lambda chunk: send_fore(chunk).wait_send())

    @pl.when(jnp.logical_not(is_first))
    def _():
        each(lambda chunk: send_fore(chunk).wait_recv())


def shards(panels, members, vectors, reflectors, inner_factors, offsets, owners):
    rows_dev, cols = vectors.shape
    blocks, basis_rows, step = reflectors.shape
    inner_rows = inner_factors.shape[1]
    per_sweep = offsets.shape[1]
    width = 256 if cols % 256 == 0 else 128
    chunks = cols // width
    units = rows_dev // step
    anywhere = pl.BlockSpec(memory_space=pl.ANY)
    dma = pltpu.SemaphoreType.DMA
    result = pl.pallas_call(
        functools.partial(kernel, panels, members, per_sweep, step, chunks, width),
        out_shape=jax.ShapeDtypeStruct((units, step, cols), jnp.float32),
        in_specs=[anywhere] * 5,
        out_specs=anywhere,
        scratch_shapes=[
            pltpu.SMEM(offsets.shape, jnp.int32),
            pltpu.SMEM(owners.shape, jnp.int32),
            pltpu.VMEM(reflectors.shape, jnp.float32),
            pltpu.VMEM(inner_factors.shape, jnp.float32),
            pltpu.VMEM((chunks, step, width), jnp.float32),
            pltpu.VMEM((chunks, units, step, width), jnp.float32),
            pltpu.VMEM((chunks, step, width), jnp.float32),
            pltpu.VMEM((4, step, width), jnp.float32),
            pltpu.VMEM((blocks, members, basis_rows + inner_rows, step), jnp.float32),
            pltpu.VMEM((blocks, step, 2 * step), jnp.bfloat16),
            pltpu.VMEM((blocks, step, 2 * step), jnp.bfloat16),
            pltpu.VMEM((blocks, 2 * step, step), jnp.bfloat16),
            pltpu.VMEM((blocks, 2 * step, step), jnp.bfloat16),
            dma((4,)),
            dma((chunks,)),
            dma((chunks,)),
            dma((chunks,)),
            dma((chunks,)),
            dma((chunks,)),
            dma((blocks, members - 1)),
            dma((blocks, members)),
            dma((chunks,)),
            dma((chunks,)),
            dma((chunks,)),
            dma((chunks,)),
        ],
        compiler_params=pltpu.CompilerParams(
            collective_id=0, has_side_effects=True, vmem_limit_bytes=60 * 1024 * 1024
        ),
        cost_estimate=pl.CostEstimate(
            flops=2 * 3 * 4 * blocks * step * step * cols,
            bytes_accessed=2 * 4 * rows_dev * cols,
            transcendentals=0,
        ),
    )(offsets, owners, vectors.reshape(units, step, cols), reflectors, inner_factors)
    return result.reshape(rows_dev, cols)


def solution(mesh):
    return jax.shard_map(
        functools.partial(shards, mesh.shape["row"], mesh.shape["vec"]),
        mesh=mesh,
        in_specs=(
            P("row", "vec"),
            P("row", "vec", None),
            P("row", "vec", None),
            P(None, "row"),
            P(None, "row"),
        ),
        out_specs=P("row", "vec"),
        check_vma=False,
    )
```

```python
import functools

import jax
import jax.numpy as jnp
from jax import lax
from jax.experimental import pallas as pl
from jax.experimental.pallas import tpu as pltpu
from jax.sharding import PartitionSpec as P

MESH = pl.DeviceIdType.MESH


def split(value):
    high = value.astype(jnp.bfloat16)
    low = (value - high.astype(jnp.float32)).astype(jnp.bfloat16)
    return high, low


def dot(left, right):
    return jnp.dot(left, right, preferred_element_type=jnp.float32)


def dot_split(left_high, left_low, right):
    right_high, right_low = split(right)
    return dot(left_high, right_high) + (dot(left_high, right_low) + dot(left_low, right_high))


def kernel(
    panels, members, per_sweep, step, chunks, width,
    offsets_in, owners_in, vectors, reflectors_in, inner_in, first_out, rest_out,
    offsets, owners, reflectors, inner, current, below, update, gathered, basis_high, basis_low, mixed_high, mixed_low,
    early_sem, load_sem, store_sem, head_sem, part_send, part_recv, back_send, back_recv, fore_send, fore_recv,
):
    panel = lax.axis_index("row")
    me = lax.axis_index("vec")
    core = lax.rem(me, 2)
    chip = me // 2
    chips = members // 2
    sibling = chip * 2 + 1 - core
    units = vectors.shape[0]
    basis_rows = reflectors.shape[1]
    first_row = panel * units * step
    is_first = panel == 0
    is_last = panel == panels - 1
    stored = [(sweep, index) for sweep in range(2) for index in range(per_sweep)]

    def columns(chunk):
        return pl.ds(pl.multiple_of(chunk * width, width), width)

    def load(chunk):
        return pltpu.make_async_copy(vectors.at[:, :, columns(chunk)], current.at[chunk], load_sem.at[chunk])

    def store(chunk):
        return pltpu.make_async_copy(
            current.at[chunk, pl.ds(1, units - 1)],
            rest_out.at[:, :, columns(chunk)],
            store_sem.at[chunk],
        )

    def store_head(chunk):
        return pltpu.make_async_copy(
            current.at[chunk, 0], head(chunk), head_sem.at[chunk]
        )

    def remote(source, target, send_sem, recv_sem, row):
        return pltpu.make_async_remote_copy(
            src_ref=source,
            dst_ref=target,
            send_sem=send_sem,
            recv_sem=recv_sem,
            device_id=(row, me),
            device_id_type=MESH,
        )

    def head(chunk):
        return first_out.at[:, columns(chunk)]

    def send_back(chunk):
        return remote(current.at[chunk, 0], below.at[chunk], back_send.at[chunk], back_recv.at[chunk], panel - 1)

    def send_fore(chunk):
        return remote(below.at[chunk], head(chunk), fore_send.at[chunk], fore_recv.at[chunk], panel + 1)

    def send_part(block, part, slot, target):
        return pltpu.make_async_remote_copy(
            src_ref=gathered.at[block, part],
            dst_ref=gathered.at[block, part],
            send_sem=part_send.at[block, slot],
            recv_sem=part_recv.at[block, part],
            device_id=(panel, target),
            device_id_type=MESH,
        )

    def other_chip(distance):
        return lax.rem(chip + distance, chips)

    def each(body):
        lax.fori_loop(0, chunks, lambda chunk, _: (body(chunk), 0)[1], 0)

    early = [
        pltpu.make_async_copy(source, target, early_sem.at[at])
        for at, (source, target) in enumerate(
            [(owners_in, owners), (offsets_in, offsets), (reflectors_in, reflectors), (inner_in, inner)]
        )
    ]
    for copy in early:
        copy.start()
    each(lambda chunk: load(chunk).start())

    barrier = pltpu.get_barrier_semaphore()

    def greet(row, vec):
        pl.semaphore_signal(barrier, inc=1, device_id=(row, vec), device_id_type=MESH)

    greet(panel, sibling)
    for distance in range(1, chips):
        greet(panel, other_chip(distance) * 2 + core)

    @pl.when(jnp.logical_not(is_first))
    def _():
        greet(panel - 1, me)

    @pl.when(jnp.logical_not(is_last))
    def _():
        greet(panel + 1, me)

    for copy in early:
        copy.wait()

    for block, (sweep, index) in enumerate(stored):
        owner = owners[sweep, index]
        gathered[block, me, :basis_rows, :] = reflectors[owner]
        gathered[block, me, basis_rows:, :] = inner[owner]

    update[0] = jnp.zeros_like(update[0])
    update[3] = jnp.zeros_like(update[3])

    beside = jnp.minimum(panel, 1) + jnp.minimum(panels - 1 - panel, 1)
    pl.semaphore_wait(barrier, chips + beside)

    for block in range(len(stored)):
        for distance in range(1, chips):
            send_part(block, me, distance, other_chip(distance) * 2 + core).start()
        send_part(block, me, 0, sibling).start()

    def fetch(block):
        for distance in range(1, chips):
            part = other_chip(distance) * 2 + core
            send_part(block, part, distance, part).wait_recv()
            send_part(block, part, chips - 1 + distance, sibling).start()
        send_part(block, sibling, 0, sibling).wait_recv()
        for distance in range(1, chips):
            part = other_chip(distance) * 2 + 1 - core
            send_part(block, part, chips - 1 + distance, sibling).wait_recv()
        basis = gathered[block, :, :basis_rows, :].reshape(2 * step, step)
        coupling = gathered[block, :, basis_rows:, :].reshape(step, step)
        high, low = split(basis)
        mixed_high[block], mixed_low[block] = split(dot_split(high, low, coupling))
        basis_high[block], basis_low[block] = split(basis.T)

    def change(block, upper, lower):
        window = jnp.concatenate([upper, lower], 0)
        projection = dot_split(basis_high[block], basis_low[block], window)
        moved = dot_split(mixed_high[block], mixed_low[block], projection)
        update[1] = moved[:step]
        update[2] = moved[step:]

    def first_unit(block):
        return jnp.maximum(offsets[stored[block][0], stored[block][1]] - first_row, 0) // step

    def lower_unit(block):
        return jnp.minimum(first_unit(block) + 1, units - 1)

    def apply_change(block, chunk, lowest):
        first = first_unit(block)
        for unit in range(lowest, units):
            place = jnp.minimum(jnp.maximum(unit + 1 - first, 0), 3)
            current[chunk, unit] = current[chunk, unit] - update[place]

    each(lambda chunk: load(chunk).wait())

    def run(block, chunk):
        change(block, current[chunk, first_unit(block)], current[chunk, lower_unit(block)])
        apply_change(block, chunk, sum(stored[block]))

    def begin(chunk):
        run(0, chunk)

        @pl.when(jnp.logical_not(is_first))
        def _():
            send_back(chunk).start()

        @pl.when(is_first)
        def _():
            store_head(chunk).start()

    last = len(stored) - 1
    fetch(0)
    each(begin)
    for block in range(1, len(stored)):
        fetch(block)

    def finish(chunk):
        for block in range(1, last):
            run(block, chunk)

        @pl.when(is_last)
        def _():
            below[chunk] = current[chunk, lower_unit(last)]

        @pl.when(jnp.logical_not(is_last))
        def _():
            send_back(chunk).wait_recv()

        change(last, current[chunk, first_unit(last)], below[chunk])

        @pl.when(jnp.logical_not(is_last))
        def _():
            below[chunk] = below[chunk] - update[2]
            send_fore(chunk).start()

        apply_change(last, chunk, per_sweep)
        store(chunk).start()

    each(finish)

    for block in range(len(stored)):
        for slot in range(members - 1):
            send_part(block, me, slot, sibling).wait_send()

    @pl.when(is_first)
    def _():
        each(lambda chunk: store_head(chunk).wait())

    @pl.when(jnp.logical_not(is_first))
    def _():
        each(lambda chunk: send_back(chunk).wait_send())

    each(lambda chunk: store(chunk).wait())

    @pl.when(jnp.logical_not(is_last))
    def _():
        each(lambda chunk: send_fore(chunk).wait_send())

    @pl.when(jnp.logical_not(is_first))
    def _():
        each(lambda chunk: send_fore(chunk).wait_recv())


def shards(panels, members, vectors, reflectors, inner_factors, offsets, owners):
    rows_dev, cols = vectors.shape
    blocks, basis_rows, step = reflectors.shape
    inner_rows = inner_factors.shape[1]
    per_sweep = offsets.shape[1]
    width = 256 if cols % 256 == 0 else 128
    chunks = cols // width
    units = rows_dev // step
    anywhere = pl.BlockSpec(memory_space=pl.ANY)
    dma = pltpu.SemaphoreType.DMA
    first, rest = pl.pallas_call(
        functools.partial(kernel, panels, members, per_sweep, step, chunks, width),
        out_shape=[
            jax.ShapeDtypeStruct((step, cols), jnp.float32),
            jax.ShapeDtypeStruct((units - 1, step, cols), jnp.float32),
        ],
        in_specs=[anywhere] * 5,
        out_specs=[anywhere] * 2,
        scratch_shapes=[
            pltpu.SMEM(offsets.shape, jnp.int32),
            pltpu.SMEM(owners.shape, jnp.int32),
            pltpu.VMEM(reflectors.shape, jnp.float32),
            pltpu.VMEM(inner_factors.shape, jnp.float32),
            pltpu.VMEM((chunks, units, step, width), jnp.float32),
            pltpu.VMEM((chunks, step, width), jnp.float32),
            pltpu.VMEM((4, step, width), jnp.float32),
            pltpu.VMEM((blocks, members, basis_rows + inner_rows, step), jnp.float32),
            pltpu.VMEM((blocks, step, 2 * step), jnp.bfloat16),
            pltpu.VMEM((blocks, step, 2 * step), jnp.bfloat16),
            pltpu.VMEM((blocks, 2 * step, step), jnp.bfloat16),
            pltpu.VMEM((blocks, 2 * step, step), jnp.bfloat16),
            dma((4,)),
            dma((chunks,)),
            dma((chunks,)),
            dma((chunks,)),
            dma((blocks, members - 1)),
            dma((blocks, members)),
            dma((chunks,)),
            dma((chunks,)),
            dma((chunks,)),
            dma((chunks,)),
        ],
        compiler_params=pltpu.CompilerParams(
            collective_id=0, has_side_effects=True, vmem_limit_bytes=60 * 1024 * 1024
        ),
        cost_estimate=pl.CostEstimate(
            flops=2 * 3 * 4 * blocks * step * step * cols,
            bytes_accessed=2 * 4 * rows_dev * cols,
            transcendentals=0,
        ),
    )(offsets, owners, vectors.reshape(units, step, cols), reflectors, inner_factors)
    return jnp.concatenate([first, rest.reshape(rows_dev - step, cols)], 0)


def solution(mesh):
    return jax.shard_map(
        functools.partial(shards, mesh.shape["row"], mesh.shape["vec"]),
        mesh=mesh,
        in_specs=(
            P("row", "vec"),
            P("row", "vec", None),
            P("row", "vec", None),
            P(None, "row"),
            P(None, "row"),
        ),
        out_specs=P("row", "vec"),
        check_vma=False,
    )
```

```python
import functools

import jax
import jax.numpy as jnp
from jax import lax
from jax.experimental import pallas as pl
from jax.experimental.pallas import tpu as pltpu
from jax.sharding import PartitionSpec as P

MESH = pl.DeviceIdType.MESH


def split(value):
    high = value.astype(jnp.bfloat16)
    low = (value - high.astype(jnp.float32)).astype(jnp.bfloat16)
    return high, low


def dot(left, right):
    return jnp.dot(left, right, preferred_element_type=jnp.float32)


def dot_split(left_high, left_low, right):
    right_high, right_low = split(right)
    return dot(left_high, right_high) + (dot(left_high, right_low) + dot(left_low, right_high))


def kernel(
    panels, members, per_sweep, step, chunks, width,
    offsets_in, owners_in, vectors, reflectors_in, inner_in, first_out, rest_out,
    offsets, owners, reflectors, inner, relay, current, below, update, gathered, basis_high, basis_low, mixed_high, mixed_low,
    early_sem, relay_send, relay_recv, load_sem, store_sem, head_sem, part_send, part_recv, back_send, back_recv, fore_send, fore_recv,
):
    panel = lax.axis_index("row")
    me = lax.axis_index("vec")
    core = lax.rem(me, 2)
    chip = me // 2
    chips = members // 2
    sibling = chip * 2 + 1 - core
    units = vectors.shape[0]
    basis_rows = reflectors.shape[1]
    first_row = panel * units * step
    is_first = panel == 0
    is_last = panel == panels - 1
    stored = [(sweep, index) for sweep in range(2) for index in range(per_sweep)]

    def columns(chunk):
        return pl.ds(pl.multiple_of(chunk * width, width), width)

    def load(chunk):
        return pltpu.make_async_copy(vectors.at[:, :, columns(chunk)], current.at[chunk], load_sem.at[chunk])

    def store(chunk):
        return pltpu.make_async_copy(
            current.at[chunk, pl.ds(1, units - 1)],
            rest_out.at[:, :, columns(chunk)],
            store_sem.at[chunk],
        )

    def store_head(chunk):
        return pltpu.make_async_copy(
            current.at[chunk, 0], first_out.at[:, columns(chunk)], head_sem.at[chunk]
        )

    half = step // 2
    pieces = 2 * chunks
    pairs = panels // 2
    is_odd = panel % 2 == 1
    pair = panel // 2

    def both(left, right):
        return jnp.logical_and(left, right)

    def back_turn(piece, source_pair):
        return piece < (pieces * (pairs - source_pair)) // pairs

    def fore_turn(piece, source_pair):
        return piece < (pieces * (source_pair + 1)) // pairs

    def remote(source, target, send_sem, recv_sem, row):
        return pltpu.make_async_remote_copy(
            src_ref=source,
            dst_ref=target,
            send_sem=send_sem,
            recv_sem=recv_sem,
            device_id=(row, me),
            device_id_type=MESH,
        )

    def top(chunk, side):
        return current.at[chunk, 0, pl.ds(side * half, half)]

    def low(chunk, side):
        return below.at[chunk, pl.ds(side * half, half)]

    def head(chunk, side):
        return first_out.at[pl.ds(side * half, half), columns(chunk)]

    def send_back(chunk, side):
        at = 2 * chunk + side
        return remote(top(chunk, side), low(chunk, side), back_send.at[at], back_recv.at[at], panel - 1)

    def send_back_far(chunk, side):
        at = 2 * chunk + side
        return remote(top(chunk, side), relay.at[at], back_send.at[at], relay_recv.at[at], panel - 2)

    def send_fore(chunk, side):
        at = 2 * chunk + side
        return remote(low(chunk, side), head(chunk, side), fore_send.at[at], fore_recv.at[at], panel + 1)

    def send_fore_far(chunk, side):
        at = 2 * chunk + side
        return remote(low(chunk, side), relay.at[at], fore_send.at[at], relay_recv.at[at], panel + 2)

    def pass_back(chunk, side):
        at = 2 * chunk + side
        return remote(relay.at[at], low(chunk, side), relay_send.at[at], back_recv.at[at], panel + 1)

    def pass_fore(chunk, side):
        at = 2 * chunk + side
        return remote(relay.at[at], head(chunk, side), relay_send.at[at], fore_recv.at[at], panel - 1)

    passes_back = both(jnp.logical_not(is_odd), panel + 2 < panels)
    passes_fore = both(is_odd, panel > 1)

    def choose(far, far_copy, near_copy):
        @pl.when(far)
        def _():
            far_copy.start()

        @pl.when(jnp.logical_not(far))
        def _():
            near_copy.start()

    def start_back(chunk):
        for side in range(2):
            far = both(jnp.logical_not(is_odd), back_turn(2 * chunk + side, pair))
            choose(far, send_back_far(chunk, side), send_back(chunk, side))

    def start_fore(chunk):
        for side in range(2):
            far = both(both(is_odd, panel + 2 < panels), fore_turn(2 * chunk + side, pair))
            choose(far, send_fore_far(chunk, side), send_fore(chunk, side))

    def hands_back(chunk, side):
        return both(passes_back, both(chunk < chunks, back_turn(2 * chunk + side, pair + 1)))

    def hands_fore(chunk, side):
        return both(passes_fore, both(chunk >= 0, fore_turn(2 * chunk + side, pair - 1)))

    def hand_back(chunk):
        for side in range(2):

            @pl.when(hands_back(chunk, side))
            def _(side=side):
                send_back_far(chunk, side).wait_recv()
                pass_back(chunk, side).start()

    def hand_fore(chunk):
        for side in range(2):

            @pl.when(hands_fore(chunk, side))
            def _(side=side):
                send_fore_far(chunk, side).wait_recv()
                pass_fore(chunk, side).start()

    def settle(chunk):
        for side in range(2):

            @pl.when(jnp.logical_or(hands_back(chunk, side), hands_fore(chunk, side)))
            def _(side=side):
                pass_back(chunk, side).wait_send()

    def sides(body):
        for side in range(2):
            body(side)

    def send_part(block, part, slot, target):
        return pltpu.make_async_remote_copy(
            src_ref=gathered.at[block, part],
            dst_ref=gathered.at[block, part],
            send_sem=part_send.at[block, slot],
            recv_sem=part_recv.at[block, part],
            device_id=(panel, target),
            device_id_type=MESH,
        )

    def other_chip(distance):
        return lax.rem(chip + distance, chips)

    def each(body):
        lax.fori_loop(0, chunks, lambda chunk, _: (body(chunk), 0)[1], 0)

    early = [
        pltpu.make_async_copy(source, target, early_sem.at[at])
        for at, (source, target) in enumerate(
            [(owners_in, owners), (offsets_in, offsets), (reflectors_in, reflectors), (inner_in, inner)]
        )
    ]
    for copy in early:
        copy.start()
    each(lambda chunk: load(chunk).start())

    barrier = pltpu.get_barrier_semaphore()

    def greet(row, vec):
        pl.semaphore_signal(barrier, inc=1, device_id=(row, vec), device_id_type=MESH)

    greet(panel, sibling)
    for distance in range(1, chips):
        greet(panel, other_chip(distance) * 2 + core)

    @pl.when(jnp.logical_not(is_first))
    def _():
        greet(panel - 1, me)

    @pl.when(jnp.logical_not(is_last))
    def _():
        greet(panel + 1, me)

    @pl.when(panel > 1)
    def _():
        greet(panel - 2, me)

    @pl.when(panel + 2 < panels)
    def _():
        greet(panel + 2, me)

    for copy in early:
        copy.wait()

    for block, (sweep, index) in enumerate(stored):
        owner = owners[sweep, index]
        gathered[block, me, :basis_rows, :] = reflectors[owner]
        gathered[block, me, basis_rows:, :] = inner[owner]

    update[0] = jnp.zeros_like(update[0])
    update[3] = jnp.zeros_like(update[3])

    beside = jnp.minimum(panel, 1) + jnp.minimum(panels - 1 - panel, 1)
    beyond = jnp.minimum(panel // 2, 1) + jnp.minimum((panels - 1 - panel) // 2, 1)
    pl.semaphore_wait(barrier, chips + beside + beyond)

    for block in range(len(stored)):
        for distance in range(1, chips):
            send_part(block, me, distance, other_chip(distance) * 2 + core).start()
        send_part(block, me, 0, sibling).start()

    def fetch(block):
        for distance in range(1, chips):
            part = other_chip(distance) * 2 + core
            send_part(block, part, distance, part).wait_recv()
            send_part(block, part, chips - 1 + distance, sibling).start()
        send_part(block, sibling, 0, sibling).wait_recv()
        for distance in range(1, chips):
            part = other_chip(distance) * 2 + 1 - core
            send_part(block, part, chips - 1 + distance, sibling).wait_recv()
        basis = gathered[block, :, :basis_rows, :].reshape(2 * step, step)
        coupling = gathered[block, :, basis_rows:, :].reshape(step, step)
        high, low = split(basis)
        mixed_high[block], mixed_low[block] = split(dot_split(high, low, coupling))
        basis_high[block], basis_low[block] = split(basis.T)

    def change(block, upper, lower):
        window = jnp.concatenate([upper, lower], 0)
        projection = dot_split(basis_high[block], basis_low[block], window)
        moved = dot_split(mixed_high[block], mixed_low[block], projection)
        update[1] = moved[:step]
        update[2] = moved[step:]

    def first_unit(block):
        return jnp.maximum(offsets[stored[block][0], stored[block][1]] - first_row, 0) // step

    def lower_unit(block):
        return jnp.minimum(first_unit(block) + 1, units - 1)

    def apply_change(block, chunk, lowest):
        first = first_unit(block)
        for unit in range(lowest, units):
            place = jnp.minimum(jnp.maximum(unit + 1 - first, 0), 3)
            current[chunk, unit] = current[chunk, unit] - update[place]

    each(lambda chunk: load(chunk).wait())

    def run(block, chunk):
        change(block, current[chunk, first_unit(block)], current[chunk, lower_unit(block)])
        apply_change(block, chunk, sum(stored[block]))

    def begin(chunk):
        run(0, chunk)

        @pl.when(jnp.logical_not(is_first))
        def _():
            start_back(chunk)

        @pl.when(is_first)
        def _():
            store_head(chunk).start()

    last = len(stored) - 1
    fetch(0)
    each(begin)
    for block in range(1, len(stored)):
        fetch(block)

    def finish(chunk):
        for block in range(1, last):
            run(block, chunk)

        hand_back(chunk + 1)

        @pl.when(is_last)
        def _():
            below[chunk] = current[chunk, lower_unit(last)]

        @pl.when(jnp.logical_not(is_last))
        def _():
            sides(lambda side: send_back(chunk, side).wait_recv())

        change(last, current[chunk, first_unit(last)], below[chunk])

        @pl.when(jnp.logical_not(is_last))
        def _():
            below[chunk] = below[chunk] - update[2]
            start_fore(chunk)

        hand_fore(chunk - 1)
        apply_change(last, chunk, per_sweep)
        store(chunk).start()

    hand_back(0)
    each(finish)
    hand_fore(chunks - 1)
    each(settle)

    for block in range(len(stored)):
        for slot in range(members - 1):
            send_part(block, me, slot, sibling).wait_send()

    @pl.when(is_first)
    def _():
        each(lambda chunk: store_head(chunk).wait())

    @pl.when(jnp.logical_not(is_first))
    def _():
        each(lambda chunk: sides(lambda side: send_back(chunk, side).wait_send()))

    each(lambda chunk: store(chunk).wait())

    @pl.when(jnp.logical_not(is_last))
    def _():
        each(lambda chunk: sides(lambda side: send_fore(chunk, side).wait_send()))

    @pl.when(jnp.logical_not(is_first))
    def _():
        each(lambda chunk: sides(lambda side: send_fore(chunk, side).wait_recv()))


def shards(panels, members, vectors, reflectors, inner_factors, offsets, owners):
    rows_dev, cols = vectors.shape
    blocks, basis_rows, step = reflectors.shape
    inner_rows = inner_factors.shape[1]
    per_sweep = offsets.shape[1]
    width = 256 if cols % 256 == 0 else 128
    chunks = cols // width
    units = rows_dev // step
    anywhere = pl.BlockSpec(memory_space=pl.ANY)
    dma = pltpu.SemaphoreType.DMA
    first, rest = pl.pallas_call(
        functools.partial(kernel, panels, members, per_sweep, step, chunks, width),
        out_shape=[
            jax.ShapeDtypeStruct((step, cols), jnp.float32),
            jax.ShapeDtypeStruct((units - 1, step, cols), jnp.float32),
        ],
        in_specs=[anywhere] * 5,
        out_specs=[anywhere] * 2,
        scratch_shapes=[
            pltpu.SMEM(offsets.shape, jnp.int32),
            pltpu.SMEM(owners.shape, jnp.int32),
            pltpu.VMEM(reflectors.shape, jnp.float32),
            pltpu.VMEM(inner_factors.shape, jnp.float32),
            pltpu.VMEM((2 * chunks, step // 2, width), jnp.float32),
            pltpu.VMEM((chunks, units, step, width), jnp.float32),
            pltpu.VMEM((chunks, step, width), jnp.float32),
            pltpu.VMEM((4, step, width), jnp.float32),
            pltpu.VMEM((blocks, members, basis_rows + inner_rows, step), jnp.float32),
            pltpu.VMEM((blocks, step, 2 * step), jnp.bfloat16),
            pltpu.VMEM((blocks, step, 2 * step), jnp.bfloat16),
            pltpu.VMEM((blocks, 2 * step, step), jnp.bfloat16),
            pltpu.VMEM((blocks, 2 * step, step), jnp.bfloat16),
            dma((4,)),
            dma((2 * chunks,)),
            dma((2 * chunks,)),
            dma((chunks,)),
            dma((chunks,)),
            dma((chunks,)),
            dma((blocks, members - 1)),
            dma((blocks, members)),
            dma((2 * chunks,)),
            dma((2 * chunks,)),
            dma((2 * chunks,)),
            dma((2 * chunks,)),
        ],
        compiler_params=pltpu.CompilerParams(
            collective_id=0, has_side_effects=True, vmem_limit_bytes=60 * 1024 * 1024
        ),
        cost_estimate=pl.CostEstimate(
            flops=2 * 3 * 4 * blocks * step * step * cols,
            bytes_accessed=2 * 4 * rows_dev * cols,
            transcendentals=0,
        ),
    )(offsets, owners, vectors.reshape(units, step, cols), reflectors, inner_factors)
    return jnp.concatenate([first, rest.reshape(rows_dev - step, cols)], 0)


def solution(mesh):
    return jax.shard_map(
        functools.partial(shards, mesh.shape["row"], mesh.shape["vec"]),
        mesh=mesh,
        in_specs=(
            P("row", "vec"),
            P("row", "vec", None),
            P("row", "vec", None),
            P(None, "row"),
            P(None, "row"),
        ),
        out_specs=P("row", "vec"),
        check_vma=False,
    )
```

```python
import functools

import jax
import jax.numpy as jnp
from jax import lax
from jax.experimental import pallas as pl
from jax.experimental.pallas import tpu as pltpu
from jax.sharding import PartitionSpec as P

MESH = pl.DeviceIdType.MESH


def split(value):
    high = value.astype(jnp.bfloat16)
    low = (value - high.astype(jnp.float32)).astype(jnp.bfloat16)
    return high, low


def dot(left, right):
    return jnp.dot(left, right, preferred_element_type=jnp.float32)


def dot_split(left_high, left_low, right):
    right_high, right_low = split(right)
    return dot(left_high, right_high) + (dot(left_high, right_low) + dot(left_low, right_high))


def kernel(
    panels, members, per_sweep, step, chunks, width,
    offsets_in, owners_in, vectors, reflectors_in, inner_in, first_out, rest_out,
    offsets, owners, reflectors, inner, current, below, update, gathered, basis_high, basis_low, mixed_high, mixed_low,
    early_sem, load_sem, store_sem, head_sem, part_send, part_recv, back_send, back_recv, fore_send, fore_recv,
):
    panel = lax.axis_index("row")
    me = lax.axis_index("vec")
    core = lax.rem(me, 2)
    chip = me // 2
    chips = members // 2
    sibling = chip * 2 + 1 - core
    units = vectors.shape[0]
    basis_rows = reflectors.shape[1]
    first_row = panel * units * step
    is_first = panel == 0
    is_last = panel == panels - 1
    stored = [(sweep, index) for sweep in range(2) for index in range(per_sweep)]

    def columns(chunk):
        return pl.ds(pl.multiple_of(chunk * width, width), width)

    def load(chunk):
        return pltpu.make_async_copy(vectors.at[:, :, columns(chunk)], current.at[chunk], load_sem.at[chunk])

    def store(chunk):
        return pltpu.make_async_copy(
            current.at[chunk, pl.ds(1, units - 1)],
            rest_out.at[:, :, columns(chunk)],
            store_sem.at[chunk],
        )

    def store_head(chunk):
        return pltpu.make_async_copy(
            current.at[chunk, 0], head(chunk), head_sem.at[chunk]
        )

    def remote(source, target, send_sem, recv_sem, row):
        return pltpu.make_async_remote_copy(
            src_ref=source,
            dst_ref=target,
            send_sem=send_sem,
            recv_sem=recv_sem,
            device_id=(row, me),
            device_id_type=MESH,
        )

    def head(chunk):
        return first_out.at[:, columns(chunk)]

    def send_back(chunk):
        return remote(current.at[chunk, 0], below.at[chunk], back_send.at[chunk], back_recv.at[chunk], panel - 1)

    def send_fore(chunk):
        return remote(below.at[chunk], head(chunk), fore_send.at[chunk], fore_recv.at[chunk], panel + 1)

    def send_part(block, part, slot, target):
        return pltpu.make_async_remote_copy(
            src_ref=gathered.at[block, part],
            dst_ref=gathered.at[block, part],
            send_sem=part_send.at[block, slot],
            recv_sem=part_recv.at[block, part],
            device_id=(panel, target),
            device_id_type=MESH,
        )

    def other_chip(distance):
        return lax.rem(chip + distance, chips)

    def each(body):
        lax.fori_loop(0, chunks, lambda chunk, _: (body(chunk), 0)[1], 0)

    early = [
        pltpu.make_async_copy(source, target, early_sem.at[at])
        for at, (source, target) in enumerate(
            [(owners_in, owners), (offsets_in, offsets), (reflectors_in, reflectors), (inner_in, inner)]
        )
    ]
    for copy in early:
        copy.start()
    each(lambda chunk: load(chunk).start())

    barrier = pltpu.get_barrier_semaphore()

    def greet(row, vec):
        pl.semaphore_signal(barrier, inc=1, device_id=(row, vec), device_id_type=MESH)

    greet(panel, sibling)
    for distance in range(1, chips):
        greet(panel, other_chip(distance) * 2 + core)

    @pl.when(jnp.logical_not(is_first))
    def _():
        greet(panel - 1, me)

    @pl.when(jnp.logical_not(is_last))
    def _():
        greet(panel + 1, me)

    for copy in early:
        copy.wait()

    for block, (sweep, index) in enumerate(stored):
        owner = owners[sweep, index]
        gathered[block, me, :basis_rows, :] = reflectors[owner]
        gathered[block, me, basis_rows:, :] = inner[owner]

    update[0] = jnp.zeros_like(update[0])
    update[3] = jnp.zeros_like(update[3])

    beside = jnp.minimum(panel, 1) + jnp.minimum(panels - 1 - panel, 1)
    pl.semaphore_wait(barrier, chips + beside)

    def spread(block):
        for distance in range(1, chips):
            send_part(block, me, distance, other_chip(distance) * 2 + core).start()
        send_part(block, me, 0, sibling).start()

    spread(0)

    def fetch(block):
        for distance in range(1, chips):
            part = other_chip(distance) * 2 + core
            send_part(block, part, distance, part).wait_recv()
            send_part(block, part, chips - 1 + distance, sibling).start()
        send_part(block, sibling, 0, sibling).wait_recv()
        for distance in range(1, chips):
            part = other_chip(distance) * 2 + 1 - core
            send_part(block, part, chips - 1 + distance, sibling).wait_recv()
        if block == 0:
            for later in range(1, len(stored)):
                spread(later)
        basis = gathered[block, :, :basis_rows, :].reshape(2 * step, step)
        coupling = gathered[block, :, basis_rows:, :].reshape(step, step)
        high, low = split(basis)
        mixed_high[block], mixed_low[block] = split(dot_split(high, low, coupling))
        basis_high[block], basis_low[block] = split(basis.T)

    def change(block, upper, lower):
        window = jnp.concatenate([upper, lower], 0)
        projection = dot_split(basis_high[block], basis_low[block], window)
        moved = dot_split(mixed_high[block], mixed_low[block], projection)
        update[1] = moved[:step]
        update[2] = moved[step:]

    def first_unit(block):
        return jnp.maximum(offsets[stored[block][0], stored[block][1]] - first_row, 0) // step

    def lower_unit(block):
        return jnp.minimum(first_unit(block) + 1, units - 1)

    def apply_change(block, chunk, lowest):
        first = first_unit(block)
        for unit in range(lowest, units):
            place = jnp.minimum(jnp.maximum(unit + 1 - first, 0), 3)
            current[chunk, unit] = current[chunk, unit] - update[place]

    each(lambda chunk: load(chunk).wait())

    def run(block, chunk):
        change(block, current[chunk, first_unit(block)], current[chunk, lower_unit(block)])
        apply_change(block, chunk, sum(stored[block]))

    def begin(chunk):
        run(0, chunk)

        @pl.when(jnp.logical_not(is_first))
        def _():
            send_back(chunk).start()

        @pl.when(is_first)
        def _():
            store_head(chunk).start()

    last = len(stored) - 1
    fetch(0)
    each(begin)
    for block in range(1, len(stored)):
        fetch(block)

    def finish(chunk):
        for block in range(1, last):
            run(block, chunk)

        @pl.when(is_last)
        def _():
            below[chunk] = current[chunk, lower_unit(last)]

        @pl.when(jnp.logical_not(is_last))
        def _():
            send_back(chunk).wait_recv()

        change(last, current[chunk, first_unit(last)], below[chunk])

        @pl.when(jnp.logical_not(is_last))
        def _():
            below[chunk] = below[chunk] - update[2]
            send_fore(chunk).start()

        apply_change(last, chunk, per_sweep)
        store(chunk).start()

    each(finish)

    for block in range(len(stored)):
        for slot in range(members - 1):
            send_part(block, me, slot, sibling).wait_send()

    @pl.when(is_first)
    def _():
        each(lambda chunk: store_head(chunk).wait())

    @pl.when(jnp.logical_not(is_first))
    def _():
        each(lambda chunk: send_back(chunk).wait_send())

    each(lambda chunk: store(chunk).wait())

    @pl.when(jnp.logical_not(is_last))
    def _():
        each(lambda chunk: send_fore(chunk).wait_send())

    @pl.when(jnp.logical_not(is_first))
    def _():
        each(lambda chunk: send_fore(chunk).wait_recv())


def shards(panels, members, vectors, reflectors, inner_factors, offsets, owners):
    rows_dev, cols = vectors.shape
    blocks, basis_rows, step = reflectors.shape
    inner_rows = inner_factors.shape[1]
    per_sweep = offsets.shape[1]
    width = 256 if cols % 256 == 0 else 128
    chunks = cols // width
    units = rows_dev // step
    anywhere = pl.BlockSpec(memory_space=pl.ANY)
    dma = pltpu.SemaphoreType.DMA
    first, rest = pl.pallas_call(
        functools.partial(kernel, panels, members, per_sweep, step, chunks, width),
        out_shape=[
            jax.ShapeDtypeStruct((step, cols), jnp.float32),
            jax.ShapeDtypeStruct((units - 1, step, cols), jnp.float32),
        ],
        in_specs=[anywhere] * 5,
        out_specs=[anywhere] * 2,
        scratch_shapes=[
            pltpu.SMEM(offsets.shape, jnp.int32),
            pltpu.SMEM(owners.shape, jnp.int32),
            pltpu.VMEM(reflectors.shape, jnp.float32),
            pltpu.VMEM(inner_factors.shape, jnp.float32),
            pltpu.VMEM((chunks, units, step, width), jnp.float32),
            pltpu.VMEM((chunks, step, width), jnp.float32),
            pltpu.VMEM((4, step, width), jnp.float32),
            pltpu.VMEM((blocks, members, basis_rows + inner_rows, step), jnp.float32),
            pltpu.VMEM((blocks, step, 2 * step), jnp.bfloat16),
            pltpu.VMEM((blocks, step, 2 * step), jnp.bfloat16),
            pltpu.VMEM((blocks, 2 * step, step), jnp.bfloat16),
            pltpu.VMEM((blocks, 2 * step, step), jnp.bfloat16),
            dma((4,)),
            dma((chunks,)),
            dma((chunks,)),
            dma((chunks,)),
            dma((blocks, members - 1)),
            dma((blocks, members)),
            dma((chunks,)),
            dma((chunks,)),
            dma((chunks,)),
            dma((chunks,)),
        ],
        compiler_params=pltpu.CompilerParams(
            collective_id=0, has_side_effects=True, vmem_limit_bytes=60 * 1024 * 1024
        ),
        cost_estimate=pl.CostEstimate(
            flops=2 * 3 * 4 * blocks * step * step * cols,
            bytes_accessed=2 * 4 * rows_dev * cols,
            transcendentals=0,
        ),
    )(offsets, owners, vectors.reshape(units, step, cols), reflectors, inner_factors)
    return jnp.concatenate([first, rest.reshape(rows_dev - step, cols)], 0)


def solution(mesh):
    return jax.shard_map(
        functools.partial(shards, mesh.shape["row"], mesh.shape["vec"]),
        mesh=mesh,
        in_specs=(
            P("row", "vec"),
            P("row", "vec", None),
            P("row", "vec", None),
            P(None, "row"),
            P(None, "row"),
        ),
        out_specs=P("row", "vec"),
        check_vma=False,
    )
```

```python
import functools

import jax
import jax.numpy as jnp
from jax import lax
from jax.experimental import pallas as pl
from jax.experimental.pallas import tpu as pltpu
from jax.sharding import PartitionSpec as P

MESH = pl.DeviceIdType.MESH


def split(value):
    high = value.astype(jnp.bfloat16)
    low = (value - high.astype(jnp.float32)).astype(jnp.bfloat16)
    return high, low


def dot(left, right):
    return jnp.dot(left, right, preferred_element_type=jnp.float32)


def dot_split(left_high, left_low, right):
    right_high, right_low = split(right)
    return dot(left_high, right_high) + (dot(left_high, right_low) + dot(left_low, right_high))


def kernel(
    panels, members, per_sweep, step, chunks, width,
    offsets_in, owners_in, vectors, reflectors_in, inner_in, first_out, rest_out,
    offsets, owners, reflectors, inner, relay, current, below, update, gathered, basis_high, basis_low, mixed_high, mixed_low,
    early_sem, relay_send, relay_recv, load_sem, store_sem, head_sem, part_send, part_recv, back_send, back_recv, fore_send, fore_recv,
):
    panel = lax.axis_index("row")
    me = lax.axis_index("vec")
    core = lax.rem(me, 2)
    chip = me // 2
    chips = members // 2
    sibling = chip * 2 + 1 - core
    units = vectors.shape[0]
    basis_rows = reflectors.shape[1]
    first_row = panel * units * step
    is_first = panel == 0
    is_last = panel == panels - 1
    stored = [(sweep, index) for sweep in range(2) for index in range(per_sweep)]

    def columns(chunk):
        return pl.ds(pl.multiple_of(chunk * width, width), width)

    def load(chunk):
        return pltpu.make_async_copy(vectors.at[:, :, columns(chunk)], current.at[chunk], load_sem.at[chunk])

    def store(chunk):
        return pltpu.make_async_copy(
            current.at[chunk, pl.ds(1, units - 1)],
            rest_out.at[:, :, columns(chunk)],
            store_sem.at[chunk],
        )

    def store_head(chunk):
        return pltpu.make_async_copy(
            current.at[chunk, 0], first_out.at[:, columns(chunk)], head_sem.at[chunk]
        )

    half = step // 2
    pieces = 2 * chunks
    pairs = panels // 2
    is_odd = panel % 2 == 1
    pair = panel // 2

    def both(left, right):
        return jnp.logical_and(left, right)

    def back_turn(piece, source_pair):
        return piece < (pieces * (pairs - source_pair)) // pairs

    def fore_turn(piece, source_pair):
        return piece < (pieces * (source_pair + 1)) // pairs

    def remote(source, target, send_sem, recv_sem, row):
        return pltpu.make_async_remote_copy(
            src_ref=source,
            dst_ref=target,
            send_sem=send_sem,
            recv_sem=recv_sem,
            device_id=(row, me),
            device_id_type=MESH,
        )

    def top(chunk, side):
        return current.at[chunk, 0, pl.ds(side * half, half)]

    def low(chunk, side):
        return below.at[chunk, pl.ds(side * half, half)]

    def head(chunk, side):
        return first_out.at[pl.ds(side * half, half), columns(chunk)]

    def send_back(chunk, side):
        at = 2 * chunk + side
        return remote(top(chunk, side), low(chunk, side), back_send.at[at], back_recv.at[at], panel - 1)

    def send_back_far(chunk, side):
        at = 2 * chunk + side
        return remote(top(chunk, side), relay.at[at], back_send.at[at], relay_recv.at[at], panel - 2)

    def send_fore(chunk, side):
        at = 2 * chunk + side
        return remote(low(chunk, side), head(chunk, side), fore_send.at[at], fore_recv.at[at], panel + 1)

    def send_fore_far(chunk, side):
        at = 2 * chunk + side
        return remote(low(chunk, side), relay.at[at], fore_send.at[at], relay_recv.at[at], panel + 2)

    def pass_back(chunk, side):
        at = 2 * chunk + side
        return remote(relay.at[at], low(chunk, side), relay_send.at[at], back_recv.at[at], panel + 1)

    def pass_fore(chunk, side):
        at = 2 * chunk + side
        return remote(relay.at[at], head(chunk, side), relay_send.at[at], fore_recv.at[at], panel - 1)

    passes_back = both(jnp.logical_not(is_odd), panel + 2 < panels)
    passes_fore = both(is_odd, panel > 1)

    def choose(far, far_copy, near_copy):
        @pl.when(far)
        def _():
            far_copy.start()

        @pl.when(jnp.logical_not(far))
        def _():
            near_copy.start()

    def start_back(chunk):
        for side in range(2):
            far = both(jnp.logical_not(is_odd), back_turn(2 * chunk + side, pair))
            choose(far, send_back_far(chunk, side), send_back(chunk, side))

    def start_fore(chunk):
        for side in range(2):
            far = both(both(is_odd, panel + 2 < panels), fore_turn(2 * chunk + side, pair))
            choose(far, send_fore_far(chunk, side), send_fore(chunk, side))

    def hands_back(chunk, side):
        return both(passes_back, both(chunk < chunks, back_turn(2 * chunk + side, pair + 1)))

    def hands_fore(chunk, side):
        return both(passes_fore, both(chunk >= 0, fore_turn(2 * chunk + side, pair - 1)))

    def hand_back(chunk):
        for side in range(2):

            @pl.when(hands_back(chunk, side))
            def _(side=side):
                send_back_far(chunk, side).wait_recv()
                pass_back(chunk, side).start()

    def hand_fore(chunk):
        for side in range(2):

            @pl.when(hands_fore(chunk, side))
            def _(side=side):
                send_fore_far(chunk, side).wait_recv()
                pass_fore(chunk, side).start()

    def settle(chunk):
        for side in range(2):

            @pl.when(jnp.logical_or(hands_back(chunk, side), hands_fore(chunk, side)))
            def _(side=side):
                pass_back(chunk, side).wait_send()

    def sides(body):
        for side in range(2):
            body(side)

    def send_part(block, part, slot, target):
        return pltpu.make_async_remote_copy(
            src_ref=gathered.at[block, part],
            dst_ref=gathered.at[block, part],
            send_sem=part_send.at[block, slot],
            recv_sem=part_recv.at[block, part],
            device_id=(panel, target),
            device_id_type=MESH,
        )

    def other_chip(distance):
        return lax.rem(chip + distance, chips)

    def each(body):
        lax.fori_loop(0, chunks, lambda chunk, _: (body(chunk), 0)[1], 0)

    early = [
        pltpu.make_async_copy(source, target, early_sem.at[at])
        for at, (source, target) in enumerate(
            [(owners_in, owners), (offsets_in, offsets), (reflectors_in, reflectors), (inner_in, inner)]
        )
    ]
    for copy in early:
        copy.start()
    each(lambda chunk: load(chunk).start())

    barrier = pltpu.get_barrier_semaphore()

    def greet(row, vec):
        pl.semaphore_signal(barrier, inc=1, device_id=(row, vec), device_id_type=MESH)

    greet(panel, sibling)
    for distance in range(1, chips):
        greet(panel, other_chip(distance) * 2 + core)

    @pl.when(jnp.logical_not(is_first))
    def _():
        greet(panel - 1, me)

    @pl.when(jnp.logical_not(is_last))
    def _():
        greet(panel + 1, me)

    @pl.when(panel > 1)
    def _():
        greet(panel - 2, me)

    @pl.when(panel + 2 < panels)
    def _():
        greet(panel + 2, me)

    for copy in early:
        copy.wait()

    for block, (sweep, index) in enumerate(stored):
        owner = owners[sweep, index]
        gathered[block, me, :basis_rows, :] = reflectors[owner]
        gathered[block, me, basis_rows:, :] = inner[owner]

    update[0] = jnp.zeros_like(update[0])
    update[3] = jnp.zeros_like(update[3])

    beside = jnp.minimum(panel, 1) + jnp.minimum(panels - 1 - panel, 1)
    beyond = jnp.minimum(panel // 2, 1) + jnp.minimum((panels - 1 - panel) // 2, 1)
    pl.semaphore_wait(barrier, chips + beside + beyond)

    def spread(block):
        for distance in range(1, chips):
            send_part(block, me, distance, other_chip(distance) * 2 + core).start()
        send_part(block, me, 0, sibling).start()

    spread(0)

    def fetch(block):
        for distance in range(1, chips):
            part = other_chip(distance) * 2 + core
            send_part(block, part, distance, part).wait_recv()
            send_part(block, part, chips - 1 + distance, sibling).start()
        send_part(block, sibling, 0, sibling).wait_recv()
        for distance in range(1, chips):
            part = other_chip(distance) * 2 + 1 - core
            send_part(block, part, chips - 1 + distance, sibling).wait_recv()
        if block == 0:
            for later in range(1, len(stored)):
                spread(later)
        basis = gathered[block, :, :basis_rows, :].reshape(2 * step, step)
        coupling = gathered[block, :, basis_rows:, :].reshape(step, step)
        high, low = split(basis)
        mixed_high[block], mixed_low[block] = split(dot_split(high, low, coupling))
        basis_high[block], basis_low[block] = split(basis.T)

    def change(block, upper, lower):
        window = jnp.concatenate([upper, lower], 0)
        projection = dot_split(basis_high[block], basis_low[block], window)
        moved = dot_split(mixed_high[block], mixed_low[block], projection)
        update[1] = moved[:step]
        update[2] = moved[step:]

    def first_unit(block):
        return jnp.maximum(offsets[stored[block][0], stored[block][1]] - first_row, 0) // step

    def lower_unit(block):
        return jnp.minimum(first_unit(block) + 1, units - 1)

    def apply_change(block, chunk, lowest):
        first = first_unit(block)
        for unit in range(lowest, units):
            place = jnp.minimum(jnp.maximum(unit + 1 - first, 0), 3)
            current[chunk, unit] = current[chunk, unit] - update[place]

    each(lambda chunk: load(chunk).wait())

    def run(block, chunk):
        change(block, current[chunk, first_unit(block)], current[chunk, lower_unit(block)])
        apply_change(block, chunk, sum(stored[block]))

    def begin(chunk):
        run(0, chunk)

        @pl.when(both(jnp.logical_not(is_first), chunk < ahead))
        def _():
            start_back(chunk)

        @pl.when(is_first)
        def _():
            store_head(chunk).start()

    last = len(stored) - 1
    ahead = 3
    fetch(0)
    each(begin)
    for block in range(1, len(stored)):
        fetch(block)

    def finish(chunk):
        @pl.when(jnp.logical_not(is_first))
        def _():
            sides(lambda side: send_back(chunk, side).wait_send())

        @pl.when(both(jnp.logical_not(is_first), chunk + ahead < chunks))
        def _():
            start_back(chunk + ahead)

        for block in range(1, last):
            run(block, chunk)

        hand_back(chunk + 1)

        @pl.when(is_last)
        def _():
            below[chunk] = current[chunk, lower_unit(last)]

        @pl.when(jnp.logical_not(is_last))
        def _():
            sides(lambda side: send_back(chunk, side).wait_recv())

        change(last, current[chunk, first_unit(last)], below[chunk])

        @pl.when(jnp.logical_not(is_last))
        def _():
            below[chunk] = below[chunk] - update[2]
            start_fore(chunk)

        hand_fore(chunk - 1)
        apply_change(last, chunk, per_sweep)
        store(chunk).start()

    hand_back(0)
    each(finish)
    hand_fore(chunks - 1)
    each(settle)

    for block in range(len(stored)):
        for slot in range(members - 1):
            send_part(block, me, slot, sibling).wait_send()

    @pl.when(is_first)
    def _():
        each(lambda chunk: store_head(chunk).wait())

    each(lambda chunk: store(chunk).wait())

    @pl.when(jnp.logical_not(is_last))
    def _():
        each(lambda chunk: sides(lambda side: send_fore(chunk, side).wait_send()))

    @pl.when(jnp.logical_not(is_first))
    def _():
        each(lambda chunk: sides(lambda side: send_fore(chunk, side).wait_recv()))


def shards(panels, members, vectors, reflectors, inner_factors, offsets, owners):
    rows_dev, cols = vectors.shape
    blocks, basis_rows, step = reflectors.shape
    inner_rows = inner_factors.shape[1]
    per_sweep = offsets.shape[1]
    width = 256 if cols % 256 == 0 else 128
    chunks = cols // width
    units = rows_dev // step
    anywhere = pl.BlockSpec(memory_space=pl.ANY)
    dma = pltpu.SemaphoreType.DMA
    first, rest = pl.pallas_call(
        functools.partial(kernel, panels, members, per_sweep, step, chunks, width),
        out_shape=[
            jax.ShapeDtypeStruct((step, cols), jnp.float32),
            jax.ShapeDtypeStruct((units - 1, step, cols), jnp.float32),
        ],
        in_specs=[anywhere] * 5,
        out_specs=[anywhere] * 2,
        scratch_shapes=[
            pltpu.SMEM(offsets.shape, jnp.int32),
            pltpu.SMEM(owners.shape, jnp.int32),
            pltpu.VMEM(reflectors.shape, jnp.float32),
            pltpu.VMEM(inner_factors.shape, jnp.float32),
            pltpu.VMEM((2 * chunks, step // 2, width), jnp.float32),
            pltpu.VMEM((chunks, units, step, width), jnp.float32),
            pltpu.VMEM((chunks, step, width), jnp.float32),
            pltpu.VMEM((4, step, width), jnp.float32),
            pltpu.VMEM((blocks, members, basis_rows + inner_rows, step), jnp.float32),
            pltpu.VMEM((blocks, step, 2 * step), jnp.bfloat16),
            pltpu.VMEM((blocks, step, 2 * step), jnp.bfloat16),
            pltpu.VMEM((blocks, 2 * step, step), jnp.bfloat16),
            pltpu.VMEM((blocks, 2 * step, step), jnp.bfloat16),
            dma((4,)),
            dma((2 * chunks,)),
            dma((2 * chunks,)),
            dma((chunks,)),
            dma((chunks,)),
            dma((chunks,)),
            dma((blocks, members - 1)),
            dma((blocks, members)),
            dma((2 * chunks,)),
            dma((2 * chunks,)),
            dma((2 * chunks,)),
            dma((2 * chunks,)),
        ],
        compiler_params=pltpu.CompilerParams(
            collective_id=0, has_side_effects=True, vmem_limit_bytes=60 * 1024 * 1024
        ),
        cost_estimate=pl.CostEstimate(
            flops=2 * 3 * 4 * blocks * step * step * cols,
            bytes_accessed=2 * 4 * rows_dev * cols,
            transcendentals=0,
        ),
    )(offsets, owners, vectors.reshape(units, step, cols), reflectors, inner_factors)
    return jnp.concatenate([first, rest.reshape(rows_dev - step, cols)], 0)


def solution(mesh):
    return jax.shard_map(
        functools.partial(shards, mesh.shape["row"], mesh.shape["vec"]),
        mesh=mesh,
        in_specs=(
            P("row", "vec"),
            P("row", "vec", None),
            P("row", "vec", None),
            P(None, "row"),
            P(None, "row"),
        ),
        out_specs=P("row", "vec"),
        check_vma=False,
    )
```
